512 devices in a mesh: replica: 64 (over x, z, y_hi), tensor: 8 (over y_lo, core).
Axes of the slice: x: 4, y: 8 (y_hi: 2, y_lo: 4; y = y_hi * 4 + y_lo), z: 8, core: 2. Of those that a mesh axis runs over, the one named last changes fastest.
Arguments:
- x_one: bfloat16 [32768, 5120], P('replica', 'tensor'), may hold values from -6 to 6
- x_two: bfloat16 [32768, 5120], P('replica', 'tensor'), may hold values from -6 to 6
- norm_one: float32 [5120], replicated, may hold values from 0.1 to 1.9
- norm_two: float32 [5120], replicated, may hold values from 0.1 to 1.9
- key_gain_one: float32 [128], replicated, may hold values from 0.1 to 1.9
- key_gain_two: float32 [128], replicated, may hold values from 0.1 to 1.9
- wk_one: bfloat16 [5120, 1024], P('replica', 'tensor'), may hold values from -0.078125 to 0.078125
- wv_one: bfloat16 [5120, 1024], P('replica', 'tensor'), may hold values from -0.078125 to 0.078125
- wk_two: bfloat16 [5120, 1024], P('replica', 'tensor'), may hold values from -0.078125 to 0.078125
- wv_two: bfloat16 [5120, 1024], P('replica', 'tensor'), may hold values from -0.078125 to 0.078125
- lengths: int32 [64], P('replica'), may hold values from 1 to 512, 24576 in all
- new_flag: int32 [64], P('replica'), may hold values from 0 to 1, as said below
- partner: int32 [64], P('replica'), may hold values from 0 to 63, as said below
Outputs:
- keys_one: bfloat16 [32768, 1024], P('replica', 'tensor')
- values_one: bfloat16 [32768, 1024], P('replica', 'tensor')
- keys_two: bfloat16 [65536, 1024], P('replica', 'tensor')
- values_two: bfloat16 [65536, 1024], P('replica', 'tensor')
The draws below stay inside these ranges and needn't reach their ends.
Inputs may be any that keep to these rules, and one draw needn't show every extreme that they name: For every slot s exactly one of new_flag[s] and new_flag[partner[s]] is 1; the first and the last slot of every aligned block of 8 slots have new_flag 0. partner[s] = s XOR 2**b, where b is 0, 1 or 2 and is the same for all slots of an aligned block of 8 slots; partner[partner[s]] = s.
All inputs are finite; a program needn't handle non-finite values. No bound on the sum of `lengths` on one device may be relied on, other than what follows from the above.
Results may differ from the reference program's by a relative error of at most 0.0049.
Values may be sent and summed in bfloat16 or wider, within the bound.
No kernel may reach another device: no remote copies, remote signals or barrier semaphores. Data moves between devices by JAX's collectives and lax.ppermute only.
A program may use at most 64 MiB of HBM per device.

```python
import math
import jax
import jax.numpy as jnp
import numpy as np
from jax import lax

D = 5120
HD = 128
ROWS = 512
KV = 1024
ALL_ROWS = 32768
N_REPLICA = 64


def pairing(key, count):
    block_bits = jax.random.randint(jax.random.fold_in(key, 11), (count // 8,), 0, 3)
    slots = jnp.arange(count, dtype=jnp.int32)
    shifted = jnp.left_shift(jnp.int32(1), jnp.repeat(block_bits, 8).astype(jnp.int32))
    partner = jnp.bitwise_xor(slots, shifted).astype(jnp.int32)
    coin = jax.random.randint(jax.random.fold_in(key, 12), (count,), 0, 2).astype(jnp.int32)
    lower = jnp.minimum(slots, partner)
    upper = jnp.maximum(slots, partner)
    low_flag = jnp.where(lower % 8 == 0, 0, jnp.where(upper % 8 == 7, 1, coin[lower]))
    flags = jnp.where(slots == lower, low_flag, 1 - low_flag)
    return (flags.astype(jnp.int32), partner)


def draw_new_flag(key, part):
    return pairing(key, N_REPLICA)[0]


def draw_partner(key, part):
    return pairing(key, N_REPLICA)[1]


def steps_of(rng, dims, shards, low, high):
    level, own = 1.0, jax.random.fold_in(rng, 6)
    for position, shards_of in shards:
        draws = jnp.exp(jax.random.uniform(jax.random.fold_in(own, position), (shards_of,), jnp.float32, low / len(shards), high / len(shards)))
        level = level * jnp.repeat(draws, dims[position] // shards_of).reshape([-1 if axis == position else 1 for axis in range(len(dims))])
    return level


def profile(number_of, total, reach, lean):
    loads = [(1 << 20) // math.isqrt(grade ** lean) + 1 for grade in range(2, number_of + 1)]
    surplus, counts = total - reach - (number_of - 1), [1] * (number_of - 1)
    while surplus > 0:
        free = [i for i in range(number_of - 1) if counts[i] < reach]
        mass, remaining = sum([loads[i] for i in free]), surplus
        for i in free:
            more = min(reach - counts[i], max(1, remaining * loads[i] // mass), surplus)
            counts[i] = counts[i] + more
            surplus = surplus - more
    return np.array([reach] + counts)


def uneven_parts(rng, count, total, limit, lean):
    if count == 2:
        one = jax.random.randint(rng, (), max(1, total - limit), min(limit, total - 1) + 1)
        return jnp.stack([one, total - one])
    sizes = jnp.asarray(profile(count, total, limit, lean), jnp.int32)
    twos = (count - 1) // 2
    donor, taker = sizes[1:1 + 2 * twos:2], sizes[2:2 + 2 * twos:2]
    room = jnp.minimum(donor - 1, limit - taker)
    moved = jax.random.randint(jax.random.fold_in(rng, 1), (twos,), 0, 1 << 20) % (room + 1)
    sizes = sizes.at[1:1 + 2 * twos:2].set(donor - moved).at[2:2 + 2 * twos:2].set(taker + moved)
    return sizes[jax.random.permutation(jax.random.fold_in(rng, 2), count)]


def gaussian(rng, extent, deviation, bound, shards=(), kind=jnp.bfloat16):
    array = jax.random.normal(rng, extent, jnp.float32) * deviation
    if len(shards) > 0:
        array = steps_of(rng, extent, shards, -0.22, 0.18) * array
    return jnp.clip(array, min=-bound, max=bound).astype(kind)


def setup_inputs(seed: int = 0) -> dict:
    seeds = jax.random.split(jax.random.key(seed), 14)
    return {
        "x_one": gaussian(seeds[0], (ALL_ROWS, D), 1.0, 6.0, ((0, 64), (1, 8))),
        "x_two": gaussian(seeds[1], (ALL_ROWS, D), 1.0, 6.0, ((0, 64), (1, 8))),
        "norm_one": jnp.clip(1.0 + 0.18 * jax.random.normal(seeds[2], (D,), jnp.float32), 0.1, 1.9),
        "norm_two": jnp.clip(1.0 + 0.18 * jax.random.normal(seeds[3], (D,), jnp.float32), 0.1, 1.9),
        "key_gain_one": jnp.clip(1.0 + 0.18 * jax.random.normal(seeds[4], (HD,), jnp.float32), 0.1, 1.9),
        "key_gain_two": jnp.clip(1.0 + 0.18 * jax.random.normal(seeds[5], (HD,), jnp.float32), 0.1, 1.9),
        "wk_one": gaussian(seeds[6], (D, KV), D ** -0.5, 0.078125, ((0, 64), (1, 8))),
        "wv_one": gaussian(seeds[7], (D, KV), D ** -0.5, 0.078125, ((0, 64), (1, 8))),
        "wk_two": gaussian(seeds[8], (D, KV), D ** -0.5, 0.078125, ((0, 64), (1, 8))),
        "wv_two": gaussian(seeds[9], (D, KV), D ** -0.5, 0.078125, ((0, 64), (1, 8))),
        "lengths": uneven_parts(seeds[10], N_REPLICA, N_REPLICA * ROWS * 3 // 4, ROWS, 1).astype(jnp.int32),
        "new_flag": draw_new_flag(jax.random.fold_in(seeds[13], 71), 0),
        "partner": draw_partner(jax.random.fold_in(seeds[13], 71), 0),
    }


def project(live, gain, w_key, w_value, key_gain):
    values = live.astype(jnp.float32)
    scale = jax.lax.rsqrt(lax.optimization_barrier(jnp.mean(values * values, axis=-1, keepdims=True)) + 1e-06)
    normed = (values * scale * gain).astype(jnp.bfloat16)
    raw_key = jnp.dot(normed, w_key, preferred_element_type=jnp.float32)
    value = jnp.dot(normed, w_value, preferred_element_type=jnp.float32)
    heads = raw_key.reshape(raw_key.shape[0], -1, HD)
    heads = heads * jax.lax.rsqrt(lax.optimization_barrier(jnp.mean(heads * heads, axis=-1, keepdims=True)) + 1e-06) * key_gain
    return (heads.reshape(raw_key.shape).astype(jnp.bfloat16), value.astype(jnp.bfloat16))

def reference(x_one, x_two, norm_one, norm_two, key_gain_one, key_gain_two, wk_one, wv_one, wk_two, wv_two, lengths, new_flag, partner):
    live_mask = (jnp.arange(ROWS, dtype=jnp.int32)[None, :] < lengths[:, None]).reshape(-1)
    live_one = jnp.where(live_mask[:, None], x_one, jnp.zeros_like(x_one))
    live_two = jnp.where(live_mask[:, None], x_two, jnp.zeros_like(x_two))
    keys_one, values_one = project(live_one, norm_one, wk_one, wv_one, key_gain_one)
    key_two, value_two = project(live_two, norm_two, wk_two, wv_two, key_gain_two)
    old = (new_flag == 0)[:, None, None]
    key_slots = key_two.reshape(N_REPLICA, ROWS, -1)
    value_slots = value_two.reshape(N_REPLICA, ROWS, -1)
    zeros = jnp.zeros_like(key_slots)
    keys_two = jnp.concatenate([jnp.where(old, key_slots, zeros), jnp.where(old, key_slots[partner], zeros)], axis=1)
    values_two = jnp.concatenate([jnp.where(old, value_slots, zeros), jnp.where(old, value_slots[partner], zeros)], axis=1)
    return (keys_one, values_one, keys_two.reshape(2 * N_REPLICA * ROWS, -1), values_two.reshape(2 * N_REPLICA * ROWS, -1))
```

```python
import functools

import jax
import jax.numpy as jnp
from jax import lax
from jax.experimental import pallas as pl
from jax.experimental.pallas import tpu as pltpu
from jax.sharding import Mesh
from jax.sharding import PartitionSpec as P

HD = 128
EPS = 1e-06
TILE = 128
AXES = ("x", "z", "h", "l", "c")
SIZES = (4, 8, 2, 4, 2)


def move(value, axes, place):
    sizes = [SIZES[AXES.index(axis)] for axis in axes]
    total = 1
    for size in sizes:
        total *= size

    def coordinates(index):
        found = []
        for size in reversed(sizes):
            found.append(index % size)
            index //= size
        return found[::-1]

    def flat(at):
        index = 0
        for size, one in zip(sizes, at):
            index = index * size + one
        return index

    pairs = [(index, flat(place(*coordinates(index)))) for index in range(total)]
    return lax.ppermute(value, axes, pairs)


def head_norm(raw_key, key_gain):
    mean = jnp.mean(raw_key * raw_key, axis=-1, keepdims=True)
    return raw_key * lax.rsqrt(mean + EPS) * key_gain


def live_scale(squares, width, length, first):
    rows = first + lax.broadcasted_iota(jnp.int32, squares.shape, 0)
    scale = lax.rsqrt(squares / width + EPS)
    return jnp.where(rows < length, scale, 0.0)


def block_of(w_ref, row, core):
    w = w_ref[pl.ds(core * 4, 4), row, 0]
    return w.reshape(w.shape[0] * w.shape[1], w.shape[2])


def two_kernel(place, *refs):
    x_refs, (w_ref, gain_ref, out_ref) = refs[:8], refs[8:]
    l, c, length = place[0], place[1], place[2]
    raw = jnp.zeros((TILE, 2 * HD), jnp.float32)
    squares = jnp.zeros((TILE, 1), jnp.float32)
    for i, x_ref in enumerate(x_refs):
        x = x_ref[...]
        w = block_of(w_ref, l ^ (i % 4), c ^ (i // 4))
        raw += jnp.dot(x, w, preferred_element_type=jnp.float32)
        wide = x.astype(jnp.float32)
        squares += jnp.sum(wide * wide, axis=-1, keepdims=True)
    raw *= live_scale(squares, 8 * x_refs[0].shape[1], length, pl.program_id(0) * TILE)
    out_ref[:, :HD] = head_norm(raw[:, :HD], gain_ref[...]).astype(out_ref.dtype)
    out_ref[:, HD:] = raw[:, HD:].astype(out_ref.dtype)


def one_kernel(place, *refs):
    x_refs, (w_ref, own_ref, other_ref, squares_ref) = refs[:4], refs[4:]
    l, c = place[0], place[1]
    mine = jnp.zeros((TILE, 2 * HD), jnp.float32)
    theirs = jnp.zeros((TILE, 2 * HD), jnp.float32)
    squares = jnp.zeros((TILE, 1), jnp.float32)
    for i, x_ref in enumerate(x_refs):
        x = x_ref[...]
        own = block_of(w_ref, l ^ (i % 2), c ^ (i // 2))
        other = block_of(w_ref, l ^ (2 + i % 2), c ^ (i // 2))
        mine += jnp.dot(x, own, preferred_element_type=jnp.float32)
        theirs += jnp.dot(x, other, preferred_element_type=jnp.float32)
        wide = x.astype(jnp.float32)
        squares += jnp.sum(wide * wide, axis=-1, keepdims=True)
    own_ref[...] = mine
    other_ref[...] = theirs.astype(other_ref.dtype)
    squares_ref[...] = jnp.broadcast_to(squares, (TILE, HD))


def finish_kernel(width, place, own_ref, other_ref, mine_ref, theirs_ref, gain_ref, key_ref, value_ref):
    raw = own_ref[...] + other_ref[...].astype(jnp.float32)
    squares = mine_ref[:, :1] + theirs_ref[:, :1]
    raw *= live_scale(squares, width, place[2], 0)
    key_ref[...] = head_norm(raw[:, :HD], gain_ref[...]).astype(key_ref.dtype)
    value_ref[...] = raw[:, HD:].astype(value_ref.dtype)


def tiled(columns):
    return pl.BlockSpec((TILE, columns), lambda step: (step, 0))


VMEM = pl.BlockSpec(memory_space=pltpu.VMEM)
SMEM = pl.BlockSpec(memory_space=pltpu.SMEM)
PARAMS = pltpu.CompilerParams(vmem_limit_bytes=40 * 1024 * 1024)


def on_device(
    x_one,
    x_two,
    norm_one,
    norm_two,
    key_gain_one,
    key_gain_two,
    wk_one,
    wv_one,
    wk_two,
    wv_two,
    lengths,
    new_flag,
    partner,
):
    rows, width = x_one.shape
    depth = wk_one.shape[0]
    x, z, h, l, c = [lax.axis_index(axis) for axis in AXES]
    slot = (x * 8 + z) * 2 + h
    place = jnp.stack([l, c, lengths[0]]).astype(jnp.int32)

    def scaled(gain, w_key, w_value):
        mine = lax.dynamic_slice(gain, (slot * depth,), (depth,))[:, None]
        both = jnp.concatenate([w_key, w_value], axis=1).astype(jnp.float32)
        return (both * mine).astype(jnp.bfloat16)

    w_one = scaled(norm_one, wk_one, wv_one)
    w_two = scaled(norm_two, wk_two, wv_two)
    one_here = move(w_one, ("x", "l"), lambda x, l: ((l & 2) | (x & 1), (x & 2) | (l & 1)))
    one_there = move(
        w_one, ("x", "h", "l"), lambda x, h, l: ((l & 2) | (x & 1), h ^ 1, (x & 2) | (l & 1))
    )
    two_there = move(w_two, ("h",), lambda h: (h ^ 1,))
    here = jnp.stack([w_two, one_here])
    there = jnp.stack([two_there, one_there])
    weights = jnp.concatenate(
        [jnp.where(h == 0, here, there), jnp.where(h == 0, there, here)], axis=1
    )
    weights = lax.all_gather(weights, "x")
    weights = lax.all_gather(weights, "z")

    def chosen(layer):
        return pl.BlockSpec((8, 4, 1, 2 * depth, 2 * HD), lambda step: (0, 0, layer, 0, 0))

    two_blocks = [x_two] + [
        move(x_two, ("l",), lambda l, apart=apart: (l ^ apart,)) for apart in (1, 2, 3)
    ]
    one_blocks = [x_one, move(x_one, ("l",), lambda l: (l ^ 1,))]
    two_blocks = two_blocks + [move(block, ("c",), lambda c: (c ^ 1,)) for block in two_blocks]
    one_blocks = one_blocks + [move(block, ("c",), lambda c: (c ^ 1,)) for block in one_blocks]

    flops = 2 * rows * 8 * width * 2 * HD
    moved = 8 * rows * width * 2 + 8 * width * 2 * HD * 2
    cost = pl.CostEstimate(flops=flops, bytes_accessed=moved, transcendentals=0)
    both_two = pl.pallas_call(
        two_kernel,
        out_shape=jax.ShapeDtypeStruct((rows, 2 * HD), jnp.bfloat16),
        grid=(rows // TILE,),
        in_specs=[SMEM] + [tiled(width)] * 8 + [chosen(0), VMEM],
        out_specs=tiled(2 * HD),
        compiler_params=PARAMS,
        cost_estimate=cost,
        name="layer_two",
    )(place, *two_blocks, weights, key_gain_two.reshape(1, HD))
    swaps = [
        move(both_two, ("z",), lambda z: (z ^ 2,)),
        move(both_two, ("h",), lambda h: (h ^ 1,)),
        move(both_two, ("z",), lambda z: (z ^ 1,)),
    ]

    own, other, squares = pl.pallas_call(
        one_kernel,
        out_shape=(
            jax.ShapeDtypeStruct((rows, 2 * HD), jnp.float32),
            jax.ShapeDtypeStruct((rows, 2 * HD), jnp.bfloat16),
            jax.ShapeDtypeStruct((rows, HD), jnp.float32),
        ),
        grid=(rows // TILE,),
        in_specs=[SMEM] + [tiled(width)] * 4 + [chosen(1)],
        out_specs=(tiled(2 * HD), tiled(2 * HD), tiled(HD)),
        compiler_params=PARAMS,
        cost_estimate=cost,
        name="layer_one",
    )(place, *one_blocks, weights)
    other = move(other, ("l",), lambda l: (l ^ 2,))
    their_squares = move(squares[:, :1].reshape(-1, HD), ("l",), lambda l: (l ^ 2,))
    their_squares = jnp.broadcast_to(their_squares.reshape(-1, 1), (rows, HD))
    keys_one, values_one = pl.pallas_call(
        functools.partial(finish_kernel, 8 * width),
        out_shape=(jax.ShapeDtypeStruct((rows, HD), jnp.bfloat16),) * 2,
        in_specs=[SMEM] + [VMEM] * 5,
        out_specs=(VMEM, VMEM),
        compiler_params=PARAMS,
        name="finish_one",
    )(place, own, other, squares, their_squares, key_gain_one.reshape(1, HD))

    pair_bit = jnp.bitwise_xor(partner[0], slot)
    received = jnp.where(pair_bit == 4, swaps[0], jnp.where(pair_bit == 1, swaps[1], swaps[2]))
    is_old = new_flag[0] == 0
    held = jnp.concatenate([both_two, received], axis=0)
    held = jnp.where(is_old, held, jnp.zeros_like(held))
    return (keys_one, values_one, held[:, :HD], held[:, HD:])


def solution(mesh):
    split = Mesh(mesh.devices.reshape(SIZES), AXES)
    whole, line = ("x", "z", "h"), ("l", "c")
    sharded = P(whole, line)
    in_specs = (sharded,) * 2 + (P(),) * 4 + (sharded,) * 4 + (P(whole),) * 3
    return jax.shard_map(
        on_device, mesh=split, in_specs=in_specs, out_specs=(sharded,) * 4, check_vma=False
    )
```

```python
import jax
import jax.numpy as jnp
from jax import lax
from jax.experimental import pallas as pl
from jax.experimental.pallas import tpu as pltpu
from jax.sharding import Mesh
from jax.sharding import PartitionSpec as P

HD = 128
EPS = 1e-06
AXES = ("x", "z", "h", "l", "c")
SIZES = (4, 8, 2, 4, 2)


def move(value, axes, place):
    sizes = [SIZES[AXES.index(axis)] for axis in axes]
    total = 1
    for size in sizes:
        total *= size

    def coordinates(index):
        found = []
        for size in reversed(sizes):
            found.append(index % size)
            index //= size
        return found[::-1]

    def flat(at):
        index = 0
        for size, one in zip(sizes, at):
            index = index * size + one
        return index

    pairs = [(index, flat(place(*coordinates(index)))) for index in range(total)]
    return lax.ppermute(value, axes, pairs)


def head_norm(raw_key, key_gain):
    mean = jnp.mean(raw_key * raw_key, axis=-1, keepdims=True)
    return raw_key * lax.rsqrt(mean + EPS) * key_gain


def row_scale(squares, width, length):
    rows = lax.broadcasted_iota(jnp.int32, squares.shape, 0)
    return jnp.where(rows < length, lax.rsqrt(squares / width + EPS), 0.0)


def copies_in(pairs, sems):
    started = [
        pltpu.make_async_copy(source, target, sems.at[i]) for i, (source, target) in enumerate(pairs)
    ]
    for copy in started:
        copy.start()
    return started


def matrix(block):
    return block.reshape(block.shape[0] * block.shape[1], block.shape[2])


def two_kernel(place, *refs):
    x_refs, (w_ref, gain_ref, out_ref, x_buf, w_buf, sems) = refs[:8], refs[8:]
    l, c, length = place[1], place[2], place[3]
    pairs = []
    for i, x_ref in enumerate(x_refs):
        cores = pl.ds((c ^ (i // 4)) * 4, 4)
        pairs.append((w_ref.at[cores, l ^ (i % 4)], w_buf.at[i]))
        pairs.append((x_ref, x_buf.at[i]))
    copies = copies_in(pairs, sems)
    raw = jnp.zeros(out_ref.shape, jnp.float32)
    squares = jnp.zeros((out_ref.shape[0], HD), jnp.float32)
    for i in range(len(x_refs)):
        copies[2 * i].wait()
        copies[2 * i + 1].wait()
        raw += jnp.dot(x_buf[i], matrix(w_buf[i]), preferred_element_type=jnp.float32)
        squares += square_sums(x_buf.at[i])
    width = len(x_refs) * x_buf.shape[2]
    raw *= row_scale(jnp.sum(squares, axis=-1, keepdims=True), width, length)
    out_ref[:, :HD] = head_norm(raw[:, :HD], gain_ref[...]).astype(out_ref.dtype)
    out_ref[:, HD:] = raw[:, HD:].astype(out_ref.dtype)


def square_sums(x_ref):
    total = jnp.zeros((x_ref.shape[0], HD), jnp.float32)
    for first in range(0, x_ref.shape[1], HD):
        wide = x_ref[:, first : first + HD].astype(jnp.float32)
        total += wide * wide
    return total


def one_kernel(place, *refs):
    x_refs, w_refs, (own_ref, other_ref, x_buf, w_buf, sems) = refs[:4], refs[4:8], refs[8:]
    x, l, c = place[0], place[1], place[2]
    pairs = []
    for half in range(2):
        cores = pl.ds((c ^ half) * 4, 4)
        pairs += [(w_ref.at[cores], w_buf.at[half, q]) for q, w_ref in enumerate(w_refs)]
        pairs += [(x_refs[2 * half + i], x_buf.at[2 * half + i]) for i in range(2)]
    copies = copies_in(pairs, sems)
    mine = jnp.zeros(own_ref.shape, jnp.float32)
    theirs = jnp.zeros(own_ref.shape, jnp.float32)
    for i in range(4):
        if i % 2 == 0:
            for copy in copies[3 * i : 3 * i + 6]:
                copy.wait()
        near = x ^ l ^ (i % 2)
        own, other = matrix(w_buf[i // 2, near]), matrix(w_buf[i // 2, near ^ 2])
        mine += jnp.dot(x_buf[i], own, preferred_element_type=jnp.float32)
        theirs += jnp.dot(x_buf[i], other, preferred_element_type=jnp.float32)
    own_ref[...] = mine
    other_ref[...] = theirs.astype(other_ref.dtype)


def finish_one_kernel(own_ref, other_ref, scale_ref, gain_ref, key_ref, value_ref):
    raw = own_ref[...] + other_ref[...].astype(jnp.float32)
    key_ref[...] = head_norm(raw[:, :HD] * scale_ref[...], gain_ref[...]).astype(key_ref.dtype)
    value_ref[...] = (raw[:, HD:] * scale_ref[...]).astype(value_ref.dtype)


def finish_two_kernel(place, own_ref, *refs):
    swap_refs, (key_ref, value_ref) = refs[:3], refs[3:]
    rows = own_ref.shape[0]
    pair_bit, is_old = place[4], place[5] == 1
    own = own_ref[...]
    received = jnp.where(pair_bit == 1, swap_refs[0][...], swap_refs[1][...])
    received = jnp.where(pair_bit == 2, swap_refs[2][...], received)
    for first, part in ((0, own), (rows, received)):
        part = jnp.where(is_old, part, jnp.zeros_like(part))
        key_ref[first : first + rows, :] = part[:, :HD]
        value_ref[first : first + rows, :] = part[:, HD:]


VMEM = pl.BlockSpec(memory_space=pltpu.VMEM)
SMEM = pl.BlockSpec(memory_space=pltpu.SMEM)
ANY = pl.BlockSpec(memory_space=pl.ANY)
PARAMS = pltpu.CompilerParams(vmem_limit_bytes=60 * 1024 * 1024)


def on_device(
    x_one,
    x_two,
    norm_one,
    norm_two,
    key_gain_one,
    key_gain_two,
    wk_one,
    wv_one,
    wk_two,
    wv_two,
    lengths,
    new_flag,
    partner,
):
    rows, width = x_one.shape
    depth = wk_one.shape[0]
    x, z, h, l, c = [lax.axis_index(axis) for axis in AXES]
    slot = (x * 8 + z) * 2 + h
    pair_bit = jnp.bitwise_xor(partner[0], slot)
    is_old = (new_flag[0] == 0).astype(jnp.int32)
    place = jnp.stack([x, l, c, lengths[0], pair_bit, is_old]).astype(jnp.int32)

    def scaled(gain, w_key, w_value):
        mine = lax.dynamic_slice(gain, (slot * depth,), (depth,))[:, None]
        both = jnp.concatenate([w_key, w_value], axis=1).astype(jnp.float32)
        return (both * mine).astype(jnp.bfloat16)

    w_one = scaled(norm_one, wk_one, wv_one)
    w_two = scaled(norm_two, wk_two, wv_two)
    two_there = move(w_two, ("h",), lambda h: (h ^ 1,))
    one_here = move(w_one, ("x", "l"), lambda x, l: ((l & 2) | (x & 1), (x & 2) | (l & 1)))
    one_there = move(
        w_one, ("x", "h", "l"), lambda x, h, l: ((l & 2) | (x & 1), h ^ 1, (x & 2) | (l & 1))
    )

    def by_h(here, there):
        return jnp.concatenate([jnp.where(h == 0, here, there), jnp.where(h == 0, there, here)])

    w_two = lax.all_gather(lax.all_gather(by_h(w_two, two_there), "x"), "z")
    w_one = lax.all_gather(by_h(one_here, one_there), "z")
    w_ones = [w_one] + [move(w_one, ("x",), lambda x, apart=apart: (x ^ apart,)) for apart in (1, 2, 3)]

    two_blocks = [x_two] + [
        move(x_two, ("l",), lambda l, apart=apart: (l ^ apart,)) for apart in (1, 2, 3)
    ]
    one_blocks = [x_one, move(x_one, ("l",), lambda l: (l ^ 1,))]
    two_blocks = two_blocks + [move(block, ("c",), lambda c: (c ^ 1,)) for block in two_blocks]
    one_blocks = one_blocks + [move(block, ("c",), lambda c: (c ^ 1,)) for block in one_blocks]

    squares = sum(jnp.sum(jnp.square(block.astype(jnp.float32)), axis=-1) for block in one_blocks)
    squares = squares.reshape(-1, HD)
    squares = squares + move(squares, ("l",), lambda l: (l ^ 2,))
    scale = row_scale(squares.reshape(-1, 1), 8 * width, lengths[0])
    scale = jnp.broadcast_to(scale, (rows, HD))
    place, scale = lax.optimization_barrier((place, scale))

    flops = 2 * rows * 8 * width * 2 * HD
    moved = 8 * rows * width * 2 + 8 * width * 2 * HD * 2
    cost = pl.CostEstimate(flops=flops, bytes_accessed=moved, transcendentals=0)
    both_two = pl.pallas_call(
        two_kernel,
        out_shape=jax.ShapeDtypeStruct((rows, 2 * HD), jnp.bfloat16),
        in_specs=[SMEM] + [ANY] * 9 + [VMEM],
        out_specs=VMEM,
        scratch_shapes=[
            pltpu.VMEM((8, rows, width), jnp.bfloat16),
            pltpu.VMEM((8, 4, 2 * depth, 2 * HD), jnp.bfloat16),
            pltpu.SemaphoreType.DMA((16,)),
        ],
        compiler_params=PARAMS,
        cost_estimate=cost,
        name="layer_two",
    )(place, *two_blocks, w_two, key_gain_two.reshape(1, HD))
    place_one, both_two = lax.optimization_barrier((place, both_two))
    swaps = [
        move(both_two, ("h",), lambda h: (h ^ 1,)),
        move(both_two, ("z",), lambda z: (z ^ 2,)),
        move(both_two, ("z",), lambda z: (z ^ 1,)),
    ]

    own, other = pl.pallas_call(
        one_kernel,
        out_shape=(
            jax.ShapeDtypeStruct((rows, 2 * HD), jnp.float32),
            jax.ShapeDtypeStruct((rows, 2 * HD), jnp.bfloat16),
        ),
        in_specs=[SMEM] + [ANY] * 8,
        out_specs=(VMEM, VMEM),
        scratch_shapes=[
            pltpu.VMEM((4, rows, width), jnp.bfloat16),
            pltpu.VMEM((2, 4, 4, 2 * depth, 2 * HD), jnp.bfloat16),
            pltpu.SemaphoreType.DMA((12,)),
        ],
        compiler_params=PARAMS,
        cost_estimate=cost,
        name="layer_one",
    )(place_one, *one_blocks, *w_ones)
    other = move(other, ("l",), lambda l: (l ^ 2,))
    keys_one, values_one = pl.pallas_call(
        finish_one_kernel,
        out_shape=(jax.ShapeDtypeStruct((rows, HD), jnp.bfloat16),) * 2,
        in_specs=[VMEM] * 4,
        out_specs=(VMEM, VMEM),
        compiler_params=PARAMS,
        name="finish_one",
    )(own, other, scale, key_gain_one.reshape(1, HD))
    keys_two, values_two = pl.pallas_call(
        finish_two_kernel,
        out_shape=(jax.ShapeDtypeStruct((2 * rows, HD), jnp.bfloat16),) * 2,
        in_specs=[SMEM] + [VMEM] * 4,
        out_specs=(VMEM, VMEM),
        compiler_params=PARAMS,
        name="finish_two",
    )(place, both_two, *swaps)
    return (keys_one, values_one, keys_two, values_two)


def solution(mesh):
    split = Mesh(mesh.devices.reshape(SIZES), AXES)
    whole, line = ("x", "z", "h"), ("l", "c")
    sharded = P(whole, line)
    in_specs = (sharded,) * 2 + (P(),) * 4 + (sharded,) * 4 + (P(whole),) * 3
    return jax.shard_map(
        on_device, mesh=split, in_specs=in_specs, out_specs=(sharded,) * 4, check_vma=False
    )
```

```python
import functools

import jax
import jax.numpy as jnp
from jax import lax
from jax.experimental import pallas as pl
from jax.experimental.pallas import tpu as pltpu
from jax.sharding import Mesh
from jax.sharding import PartitionSpec as P

HD = 128
EPS = 1e-06
TILE = 128
AXES = ("x", "z", "h", "l", "c")
SIZES = (4, 8, 2, 4, 2)


def move(value, axes, place):
    sizes = [SIZES[AXES.index(axis)] for axis in axes]
    total = 1
    for size in sizes:
        total *= size

    def coordinates(index):
        found = []
        for size in reversed(sizes):
            found.append(index % size)
            index //= size
        return found[::-1]

    def flat(at):
        index = 0
        for size, one in zip(sizes, at):
            index = index * size + one
        return index

    pairs = [(index, flat(place(*coordinates(index)))) for index in range(total)]
    return lax.ppermute(value, axes, pairs)


def head_norm(raw_key, key_gain):
    mean = jnp.mean(raw_key * raw_key, axis=-1, keepdims=True)
    return raw_key * lax.rsqrt(mean + EPS) * key_gain


def row_scale(squares, width, live):
    return jnp.where(live, lax.rsqrt(squares / width + EPS), 0.0)


def square_sums(x):
    wide = x.astype(jnp.float32)
    wide = wide * wide
    return sum(wide[:, first : first + HD] for first in range(0, x.shape[1], HD))


def joined(blocks, weights):
    x = jnp.concatenate([block[...] for block in blocks], axis=1)
    w = jnp.concatenate([w.reshape(-1, w.shape[-1]) for w in weights])
    return jnp.dot(x, w, preferred_element_type=jnp.float32)


def squares_kernel(near, near1, far3, far2, squares_ref):
    blocks = [near.at[1], near1.at[1], far2, far3]
    squares_ref[...] = sum(square_sums(block[...]) for block in blocks)


def two_kernel(place, near, near1, far3, far2, near_c, near1_c, far3_c, far2_c, *refs):
    squares_ref, w_ref, gain_ref, out_ref = refs
    l, c = place[1], place[2]
    blocks = [near.at[1], near1.at[1], far2, far3, near_c.at[1], near1_c.at[1], far2_c, far3_c]

    def weights(i):
        return w_ref[pl.ds((c ^ (i // 4)) * 4, 4), l ^ (i % 4), 0]

    raw = sum(joined(blocks[i : i + 2], [weights(i), weights(i + 1)]) for i in (0, 2, 4, 6))
    squares = squares_ref[...] + sum(square_sums(block[...]) for block in blocks[4:])
    squares = jnp.sum(squares, axis=-1, keepdims=True)
    live = lax.broadcasted_iota(jnp.int32, squares.shape, 0) < place[3]
    raw *= row_scale(squares, len(blocks) * far2.shape[1], live)
    out_ref[:, :HD] = head_norm(raw[:, :HD], gain_ref[...]).astype(out_ref.dtype)
    out_ref[:, HD:] = raw[:, HD:].astype(out_ref.dtype)


def one_kernel(place, near, near1, near_c, near1_c, *refs):
    w_ref, own_ref, other_ref, squares_ref = refs
    l, c = place[1], place[2]
    blocks = [near.at[0], near1.at[0], near_c.at[0], near1_c.at[0]]
    squares = sum(square_sums(block[...]) for block in blocks)

    def product(side):
        total = 0.0
        for core in range(2):
            cores = pl.ds((c ^ core) * 4, 4)
            weights = [w_ref[cores, l ^ side, 1], w_ref[cores, l ^ side ^ 1, 1]]
            total += joined(blocks[2 * core : 2 * core + 2], weights)
        return total

    own_ref[...] = product(0)
    other = product(2)
    rows = own_ref.shape[0]
    other_ref[:rows, :] = other.astype(other_ref.dtype)
    for first in range(0, rows, TILE):
        line = jnp.sum(squares[first : first + TILE].T, axis=0, keepdims=True)
        squares_ref[first // TILE : first // TILE + 1, :] = line
    squares = squares_ref[...]
    high = squares.astype(other_ref.dtype).astype(jnp.float32)
    tail = jnp.concatenate([high, squares - high], axis=1)
    tail = jnp.concatenate([tail, jnp.zeros((16 - tail.shape[0], 2 * HD), jnp.float32)])
    other_ref[rows : rows + 16, :] = tail.astype(other_ref.dtype)


def finish_one_kernel(width, place, own_ref, other_ref, squares_ref, gain_ref, key_ref, value_ref):
    rows_all = own_ref.shape[0]
    theirs = other_ref[rows_all : rows_all + 16, :].astype(jnp.float32)
    for first in range(0, rows_all, TILE):
        rows = slice(first, first + TILE)
        step = first // TILE
        line = squares_ref[step : step + 1, :] + theirs[step : step + 1, :HD]
        line += theirs[step : step + 1, HD:]
        live = first + lax.broadcasted_iota(jnp.int32, line.shape, 1) < place[3]
        scale = jnp.broadcast_to(row_scale(line, width, live), (HD, TILE)).T
        raw = own_ref[rows, :] + other_ref[rows, :].astype(jnp.float32)
        key_ref[rows, :] = head_norm(raw[:, :HD] * scale, gain_ref[...]).astype(key_ref.dtype)
        value_ref[rows, :] = (raw[:, HD:] * scale).astype(value_ref.dtype)


def finish_two_kernel(place, own_ref, *refs):
    swap_refs, (key_ref, value_ref) = refs[:3], refs[3:]
    rows = own_ref.shape[0]
    pair_bit, is_old = place[4], place[5] == 1
    own = own_ref[...]
    received = jnp.where(pair_bit == 2, swap_refs[0][...], swap_refs[1][...])
    received = jnp.where(pair_bit == 1, swap_refs[2][...], received)
    for first, part in ((0, own), (rows, received)):
        part = jnp.where(is_old, part, jnp.zeros_like(part))
        key_ref[first : first + rows, :] = part[:, :HD]
        value_ref[first : first + rows, :] = part[:, HD:]


VMEM = pl.BlockSpec(memory_space=pltpu.VMEM)
SMEM = pl.BlockSpec(memory_space=pltpu.SMEM)
PARAMS = pltpu.CompilerParams(vmem_limit_bytes=24 * 1024 * 1024)


def on_device(
    x_one,
    x_two,
    norm_one,
    norm_two,
    key_gain_one,
    key_gain_two,
    wk_one,
    wv_one,
    wk_two,
    wv_two,
    lengths,
    new_flag,
    partner,
):
    rows, width = x_one.shape
    depth = wk_one.shape[0]
    x, z, h, l, c = [lax.axis_index(axis) for axis in AXES]
    slot = (x * 8 + z) * 2 + h
    pair_bit = jnp.bitwise_xor(partner[0], slot)
    is_old = (new_flag[0] == 0).astype(jnp.int32)
    def scaled(gain, w_key, w_value):
        mine = lax.dynamic_slice(gain, (slot * depth,), (depth,))[:, None]
        both = jnp.concatenate([w_key, w_value], axis=1).astype(jnp.float32)
        return (both * mine).astype(jnp.bfloat16)

    w_one = scaled(norm_one, wk_one, wv_one)
    w_two = scaled(norm_two, wk_two, wv_two)
    two_there = move(w_two, ("h",), lambda h: (h ^ 1,))
    one_here = move(w_one, ("x", "l"), lambda x, l: ((l & 2) | (x & 1), (x & 2) | (l & 1)))
    one_there = move(
        w_one, ("x", "h", "l"), lambda x, h, l: ((l & 2) | (x & 1), h ^ 1, (x & 2) | (l & 1))
    )

    def by_h(here, there):
        return jnp.concatenate([jnp.where(h == 0, here, there), jnp.where(h == 0, there, here)])

    weights = jnp.stack([by_h(w_two, two_there), by_h(one_here, one_there)])
    weights = lax.all_gather(weights, "x")
    weights = lax.all_gather(weights, "z")

    def swapped(block):
        return move(block, ("c",), lambda c: (c ^ 1,))

    near = jnp.stack([x_one, x_two])
    near1 = move(near, ("l",), lambda l: (l ^ 1,))
    far3 = move(x_two, ("l",), lambda l: (l ^ 3,))
    far2 = move(x_two, ("l",), lambda l: (l ^ 2,))
    near1, far2 = lax.optimization_barrier((near1, far2))
    two_blocks = [near, near1, far3, far2]
    two_blocks += [swapped(block) for block in two_blocks]
    one_blocks = [two_blocks[i] for i in (0, 1, 4, 5)]
    place = jnp.stack([x, l, c, lengths[0], pair_bit, is_old]).astype(jnp.int32)

    flops = 2 * rows * 8 * width * 2 * HD
    moved = 8 * rows * width * 2 + 8 * width * 2 * HD * 2
    cost = pl.CostEstimate(flops=flops, bytes_accessed=moved, transcendentals=0)
    squares_two = pl.pallas_call(
        squares_kernel,
        out_shape=jax.ShapeDtypeStruct((rows, HD), jnp.float32),
        in_specs=[VMEM] * 4,
        out_specs=VMEM,
        compiler_params=PARAMS,
        cost_estimate=pl.CostEstimate(flops=1_000_000_000, bytes_accessed=0, transcendentals=0),
        name="squares_two",
    )(*two_blocks[:4])
    both_two = pl.pallas_call(
        two_kernel,
        out_shape=jax.ShapeDtypeStruct((rows, 2 * HD), jnp.bfloat16),
        in_specs=[SMEM] + [VMEM] * 11,
        out_specs=VMEM,
        compiler_params=PARAMS,
        cost_estimate=cost,
        name="layer_two",
    )(place, *two_blocks, squares_two, weights, key_gain_two.reshape(1, HD))
    place, both_two = lax.optimization_barrier((place, both_two))
    swaps = [
        move(both_two, ("z",), lambda z: (z ^ 1,)),
        move(both_two, ("z",), lambda z: (z ^ 2,)),
        move(both_two, ("h",), lambda h: (h ^ 1,)),
    ]

    own, other, squares = pl.pallas_call(
        one_kernel,
        out_shape=(
            jax.ShapeDtypeStruct((rows, 2 * HD), jnp.float32),
            jax.ShapeDtypeStruct((rows + 16, 2 * HD), jnp.bfloat16),
            jax.ShapeDtypeStruct((rows // TILE, HD), jnp.float32),
        ),
        in_specs=[SMEM] + [VMEM] * 5,
        out_specs=(VMEM, VMEM, VMEM),
        compiler_params=PARAMS,
        cost_estimate=cost,
        name="layer_one",
    )(place, *one_blocks, weights)
    other = move(other, ("l",), lambda l: (l ^ 2,))
    keys_one, values_one = pl.pallas_call(
        functools.partial(finish_one_kernel, 8 * width),
        out_shape=(jax.ShapeDtypeStruct((rows, HD), jnp.bfloat16),) * 2,
        in_specs=[SMEM] + [VMEM] * 4,
        out_specs=(VMEM, VMEM),
        compiler_params=PARAMS,
        name="finish_one",
    )(place, own, other, squares, key_gain_one.reshape(1, HD))
    keys_two, values_two = pl.pallas_call(
        finish_two_kernel,
        out_shape=(jax.ShapeDtypeStruct((2 * rows, HD), jnp.bfloat16),) * 2,
        in_specs=[SMEM] + [VMEM] * 4,
        out_specs=(VMEM, VMEM),
        compiler_params=PARAMS,
        name="finish_two",
    )(place, both_two, *swaps)
    return (keys_one, values_one, keys_two, values_two)


def solution(mesh):
    split = Mesh(mesh.devices.reshape(SIZES), AXES)
    whole, line = ("x", "z", "h"), ("l", "c")
    sharded = P(whole, line)
    in_specs = (sharded,) * 2 + (P(),) * 4 + (sharded,) * 4 + (P(whole),) * 3
    return jax.shard_map(
        on_device, mesh=split, in_specs=in_specs, out_specs=(sharded,) * 4, check_vma=False
    )
```

```python
import jax
import jax.numpy as jnp
from jax import lax
from jax.experimental import pallas as pl
from jax.experimental.pallas import tpu as pltpu
from jax.sharding import Mesh
from jax.sharding import PartitionSpec as P

HD = 128
EPS = 1e-06
AXES = ("x", "z", "h", "l", "c")
SIZES = (4, 8, 2, 4, 2)


def move(value, axes, place):
    sizes = [SIZES[AXES.index(axis)] for axis in axes]
    total = 1
    for size in sizes:
        total *= size

    def coordinates(index):
        found = []
        for size in reversed(sizes):
            found.append(index % size)
            index //= size
        return found[::-1]

    def flat(at):
        index = 0
        for size, one in zip(sizes, at):
            index = index * size + one
        return index

    pairs = [(index, flat(place(*coordinates(index)))) for index in range(total)]
    return lax.ppermute(value, axes, pairs)


def head_norm(raw_key, key_gain):
    mean = jnp.mean(raw_key * raw_key, axis=-1, keepdims=True)
    return raw_key * lax.rsqrt(mean + EPS) * key_gain


def row_scale(squares, width, live):
    return jnp.where(live, lax.rsqrt(squares / width + EPS), 0.0)


def square_sums(x):
    wide = x.astype(jnp.float32)
    wide = wide * wide
    return sum(wide[:, first : first + HD] for first in range(0, x.shape[1], HD))


def project(place, layer, x_refs, w_ref, gain_ref, squares=0.0):
    l, c, length = place[0], place[1], place[2]
    raw = 0.0
    known = len(x_refs) // 2 if isinstance(squares, jax.Array) else 0
    for i in range(0, len(x_refs), 2):
        x = jnp.concatenate([x_ref[...] for x_ref in x_refs[i : i + 2]], axis=1)
        cores = pl.ds((c ^ (i // 4)) * 4, 4)
        w = [w_ref[cores, l ^ (i % 4), layer], w_ref[cores, l ^ (i % 4 + 1), layer]]
        w = jnp.concatenate([half.reshape(-1, 2 * HD) for half in w])
        raw += jnp.dot(x, w, preferred_element_type=jnp.float32)
        if i >= known:
            squares += square_sums(x)
    squares = jnp.sum(squares, axis=-1, keepdims=True)
    live = lax.broadcasted_iota(jnp.int32, squares.shape, 0) < length
    raw *= row_scale(squares, len(x_refs) * x_refs[0].shape[1], live)
    return head_norm(raw[:, :HD], gain_ref[...]).astype(jnp.bfloat16), raw[:, HD:].astype(jnp.bfloat16)


def squares_kernel(*refs):
    refs[-1][...] = sum(square_sums(x_ref[...]) for x_ref in refs[:-1])


def one_kernel(place, *refs):
    key_ref, value_ref = refs[10:]
    key_ref[...], value_ref[...] = project(place, 0, refs[:8], refs[8], refs[9])


def two_kernel(place, *refs):
    out_ref = refs[11]
    keys, values = project(place, 1, refs[:8], refs[8], refs[9], refs[10][...])
    out_ref[:, :HD], out_ref[:, HD:] = keys, values


def finish_two_kernel(place, own_ref, *refs):
    swap_refs, (key_ref, value_ref) = refs[:3], refs[3:]
    rows = own_ref.shape[0]
    pair_bit, is_old = place[3], place[4] == 1
    own = own_ref[...]
    received = jnp.where(pair_bit == 1, swap_refs[0][...], swap_refs[1][...])
    received = jnp.where(pair_bit == 2, swap_refs[2][...], received)
    for first, part in ((0, own), (rows, received)):
        part = jnp.where(is_old, part, jnp.zeros_like(part))
        key_ref[first : first + rows, :] = part[:, :HD]
        value_ref[first : first + rows, :] = part[:, HD:]


VMEM = pl.BlockSpec(memory_space=pltpu.VMEM)
SMEM = pl.BlockSpec(memory_space=pltpu.SMEM)
PARAMS = pltpu.CompilerParams(vmem_limit_bytes=24 * 1024 * 1024)


def on_device(
    x_one,
    x_two,
    norm_one,
    norm_two,
    key_gain_one,
    key_gain_two,
    wk_one,
    wv_one,
    wk_two,
    wv_two,
    lengths,
    new_flag,
    partner,
):
    rows, width = x_one.shape
    depth = wk_one.shape[0]
    x, z, h, l, c = [lax.axis_index(axis) for axis in AXES]
    slot = (x * 8 + z) * 2 + h
    pair_bit = jnp.bitwise_xor(partner[0], slot)
    is_old = (new_flag[0] == 0).astype(jnp.int32)
    def scaled(gain, w_key, w_value):
        mine = lax.dynamic_slice(gain, (slot * depth,), (depth,))[:, None]
        both = jnp.concatenate([w_key, w_value], axis=1).astype(jnp.float32)
        return (both * mine).astype(jnp.bfloat16)

    here = jnp.stack([scaled(norm_one, wk_one, wv_one), scaled(norm_two, wk_two, wv_two)])
    there = move(here, ("h",), lambda h: (h ^ 1,))
    weights = jnp.concatenate(
        [jnp.where(h == 0, here, there), jnp.where(h == 0, there, here)], axis=1
    )
    weights = lax.all_gather(lax.all_gather(weights, "x"), "z")

    def from_line(block, apart):
        return move(block, ("l",), lambda l: (l ^ apart,))

    def from_core(block):
        return move(block, ("c",), lambda c: (c ^ 1,))

    two_far = from_line(x_two, 2)
    two_near = from_line(x_two, 1)
    two_blocks = [x_two, two_near, two_far, from_line(two_far, 1)]
    squares_two = pl.pallas_call(
        squares_kernel,
        out_shape=jax.ShapeDtypeStruct((rows, HD), jnp.float32),
        in_specs=[VMEM] * 4,
        out_specs=VMEM,
        compiler_params=PARAMS,
        cost_estimate=pl.CostEstimate(flops=90_000_000_000, bytes_accessed=0, transcendentals=0),
        name="squares_two",
    )(*two_blocks)
    two_blocks += [from_core(block) for block in two_blocks]
    x_first, two_far = lax.optimization_barrier((x_one, two_far))
    one_near, one_far = from_line(x_first, 1), from_line(x_first, 2)
    one_near, one_far = lax.optimization_barrier((one_near, one_far))
    one_last = from_line(one_far, 1)
    place = jnp.stack([l, c, lengths[0], pair_bit, is_old]).astype(jnp.int32)

    flops = 2 * rows * 8 * width * 2 * HD
    moved = 8 * rows * width * 2 + 8 * width * 2 * HD * 2
    cost = pl.CostEstimate(flops=flops, bytes_accessed=moved, transcendentals=0)
    both_two = pl.pallas_call(
        two_kernel,
        out_shape=jax.ShapeDtypeStruct((rows, 2 * HD), jnp.bfloat16),
        in_specs=[SMEM] + [VMEM] * 11,
        out_specs=VMEM,
        compiler_params=PARAMS,
        cost_estimate=cost,
        name="layer_two",
    )(place, *two_blocks, weights, key_gain_two.reshape(1, HD), squares_two)
    swaps = [
        move(both_two, ("h",), lambda h: (h ^ 1,)),
        move(both_two, ("z",), lambda z: (z ^ 2,)),
        move(both_two, ("z",), lambda z: (z ^ 1,)),
    ]

    one_last, both_two = lax.optimization_barrier((one_last, both_two))
    one_blocks = [x_one, one_near, one_far, one_last]
    one_blocks += [from_core(block) for block in one_blocks]
    keys_one, values_one = pl.pallas_call(
        one_kernel,
        out_shape=(jax.ShapeDtypeStruct((rows, HD), jnp.bfloat16),) * 2,
        in_specs=[SMEM] + [VMEM] * 10,
        out_specs=(VMEM, VMEM),
        compiler_params=PARAMS,
        cost_estimate=cost,
        name="layer_one",
    )(place, *one_blocks, weights, key_gain_one.reshape(1, HD))
    place, keys_one, values_one = lax.optimization_barrier((place, keys_one, values_one))
    keys_two, values_two = pl.pallas_call(
        finish_two_kernel,
        out_shape=(jax.ShapeDtypeStruct((2 * rows, HD), jnp.bfloat16),) * 2,
        in_specs=[SMEM] + [VMEM] * 4,
        out_specs=(VMEM, VMEM),
        compiler_params=PARAMS,
        name="finish_two",
    )(place, both_two, *swaps)
    return (keys_one, values_one, keys_two, values_two)


def solution(mesh):
    split = Mesh(mesh.devices.reshape(SIZES), AXES)
    whole, line = ("x", "z", "h"), ("l", "c")
    sharded = P(whole, line)
    in_specs = (sharded,) * 2 + (P(),) * 4 + (sharded,) * 4 + (P(whole),) * 3
    return jax.shard_map(
        on_device, mesh=split, in_specs=in_specs, out_specs=(sharded,) * 4, check_vma=False
    )
```

```python
import jax
import jax.numpy as jnp
from jax import lax
from jax.experimental import pallas as pl
from jax.experimental.pallas import tpu as pltpu
from jax.sharding import Mesh
from jax.sharding import PartitionSpec as P

HD = 128
EPS = 1e-06
AXES = ("x", "z", "h", "l", "c")
SIZES = (4, 8, 2, 4, 2)


def move(value, axes, place):
    sizes = [SIZES[AXES.index(axis)] for axis in axes]
    total = 1
    for size in sizes:
        total *= size

    def coordinates(index):
        found = []
        for size in reversed(sizes):
            found.append(index % size)
            index //= size
        return found[::-1]

    def flat(at):
        index = 0
        for size, one in zip(sizes, at):
            index = index * size + one
        return index

    pairs = [(index, flat(place(*coordinates(index)))) for index in range(total)]
    return lax.ppermute(value, axes, pairs)


def head_norm(raw_key, key_gain):
    mean = jnp.mean(raw_key * raw_key, axis=-1, keepdims=True)
    return raw_key * lax.rsqrt(mean + EPS) * key_gain


def row_scale(squares, width, live):
    return jnp.where(live, lax.rsqrt(squares / width + EPS), 0.0)


def square_sums(x):
    wide = x.astype(jnp.float32)
    wide = wide * wide
    return sum(wide[:, first : first + HD] for first in range(0, x.shape[1], HD))


def project(place, layer, x_refs, w_ref, gain_ref, squares=0.0):
    l, c, length = place[0], place[1], place[2]
    raw = 0.0
    known = len(x_refs) // 2 if isinstance(squares, jax.Array) else 0
    for i in range(0, len(x_refs), 2):
        x = jnp.concatenate([x_ref[...] for x_ref in x_refs[i : i + 2]], axis=1)
        cores = pl.ds((c ^ (i // 4)) * 4, 4)
        w = [w_ref[cores, l ^ (i % 4), layer], w_ref[cores, l ^ (i % 4 + 1), layer]]
        w = jnp.concatenate([half.reshape(-1, 2 * HD) for half in w])
        raw += jnp.dot(x, w, preferred_element_type=jnp.float32)
        if i >= known:
            squares += square_sums(x)
    squares = jnp.sum(squares, axis=-1, keepdims=True)
    live = lax.broadcasted_iota(jnp.int32, squares.shape, 0) < length
    raw *= row_scale(squares, len(x_refs) * x_refs[0].shape[1], live)
    return head_norm(raw[:, :HD], gain_ref[...]).astype(jnp.bfloat16), raw[:, HD:].astype(jnp.bfloat16)


def squares_kernel(*refs):
    refs[-1][...] = sum(square_sums(x_ref[...]) for x_ref in refs[:-1])


def one_kernel(place, *refs):
    key_ref, value_ref = refs[10:]
    key_ref[...], value_ref[...] = project(place, 0, refs[:8], refs[8], refs[9])


def two_kernel(place, *refs):
    out_ref = refs[11]
    keys, values = project(place, 1, refs[:8], refs[8], refs[9], refs[10][...])
    out_ref[:, :HD], out_ref[:, HD:] = keys, values


def finish_two_kernel(place, own_ref, *refs):
    swap_refs, (key_ref, value_ref) = refs[:3], refs[3:]
    rows = own_ref.shape[0]
    pair_bit, is_old = place[3], place[4] == 1
    own = own_ref[...]
    received = jnp.where(pair_bit == 1, swap_refs[0][...], swap_refs[1][...])
    received = jnp.where(pair_bit == 2, swap_refs[2][...], received)
    for first, part in ((0, own), (rows, received)):
        part = jnp.where(is_old, part, jnp.zeros_like(part))
        key_ref[first : first + rows, :] = part[:, :HD]
        value_ref[first : first + rows, :] = part[:, HD:]


VMEM = pl.BlockSpec(memory_space=pltpu.VMEM)
SMEM = pl.BlockSpec(memory_space=pltpu.SMEM)
PARAMS = pltpu.CompilerParams(vmem_limit_bytes=24 * 1024 * 1024)


def on_device(
    x_one,
    x_two,
    norm_one,
    norm_two,
    key_gain_one,
    key_gain_two,
    wk_one,
    wv_one,
    wk_two,
    wv_two,
    lengths,
    new_flag,
    partner,
):
    rows, width = x_one.shape
    depth = wk_one.shape[0]
    x, z, h, l, c = [lax.axis_index(axis) for axis in AXES]
    slot = (x * 8 + z) * 2 + h
    pair_bit = jnp.bitwise_xor(partner[0], slot)
    is_old = (new_flag[0] == 0).astype(jnp.int32)
    def scaled(gain, w_key, w_value):
        mine = lax.dynamic_slice(gain, (slot * depth,), (depth,))[:, None]
        both = jnp.concatenate([w_key, w_value], axis=1).astype(jnp.float32)
        return (both * mine).astype(jnp.bfloat16)

    here = jnp.stack([scaled(norm_one, wk_one, wv_one), scaled(norm_two, wk_two, wv_two)])
    there = move(here, ("h",), lambda h: (h ^ 1,))
    weights = jnp.concatenate(
        [jnp.where(h == 0, here, there), jnp.where(h == 0, there, here)], axis=1
    )
    weights = lax.all_gather(lax.all_gather(weights, "x"), "z")

    def from_line(block, apart):
        return move(block, ("l",), lambda l: (l ^ apart,))

    def from_core(block):
        return move(block, ("c",), lambda c: (c ^ 1,))

    two_far = from_line(x_two, 2)
    two_near = from_line(x_two, 1)
    two_blocks = [x_two, two_near, two_far, from_line(two_far, 1)]
    squares_two = pl.pallas_call(
        squares_kernel,
        out_shape=jax.ShapeDtypeStruct((rows, HD), jnp.float32),
        in_specs=[VMEM] * 4,
        out_specs=VMEM,
        compiler_params=PARAMS,
        cost_estimate=pl.CostEstimate(flops=90_000_000_000, bytes_accessed=0, transcendentals=0),
        name="squares_two",
    )(*two_blocks)
    two_blocks += [from_core(block) for block in two_blocks]
    one_far = from_line(x_one, 2)
    x_first, two_near = lax.optimization_barrier((x_one, two_near))
    one_near = from_line(x_first, 1)
    one_last = from_line(one_far, 1)
    place = jnp.stack([l, c, lengths[0], pair_bit, is_old]).astype(jnp.int32)

    flops = 2 * rows * 8 * width * 2 * HD
    moved = 8 * rows * width * 2 + 8 * width * 2 * HD * 2
    cost = pl.CostEstimate(flops=flops, bytes_accessed=moved, transcendentals=0)
    both_two = pl.pallas_call(
        two_kernel,
        out_shape=jax.ShapeDtypeStruct((rows, 2 * HD), jnp.bfloat16),
        in_specs=[SMEM] + [VMEM] * 11,
        out_specs=VMEM,
        compiler_params=PARAMS,
        cost_estimate=cost,
        name="layer_two",
    )(place, *two_blocks, weights, key_gain_two.reshape(1, HD), squares_two)
    swaps = [
        move(both_two, ("h",), lambda h: (h ^ 1,)),
        move(both_two, ("z",), lambda z: (z ^ 2,)),
        move(both_two, ("z",), lambda z: (z ^ 1,)),
    ]

    one_last, both_two = lax.optimization_barrier((one_last, both_two))
    one_blocks = [x_one, one_near, one_far, one_last]
    one_blocks += [from_core(block) for block in one_blocks]
    keys_one, values_one = pl.pallas_call(
        one_kernel,
        out_shape=(jax.ShapeDtypeStruct((rows, HD), jnp.bfloat16),) * 2,
        in_specs=[SMEM] + [VMEM] * 10,
        out_specs=(VMEM, VMEM),
        compiler_params=PARAMS,
        cost_estimate=cost,
        name="layer_one",
    )(place, *one_blocks, weights, key_gain_one.reshape(1, HD))
    place, keys_one, values_one = lax.optimization_barrier((place, keys_one, values_one))
    keys_two, values_two = pl.pallas_call(
        finish_two_kernel,
        out_shape=(jax.ShapeDtypeStruct((2 * rows, HD), jnp.bfloat16),) * 2,
        in_specs=[SMEM] + [VMEM] * 4,
        out_specs=(VMEM, VMEM),
        compiler_params=PARAMS,
        name="finish_two",
    )(place, both_two, *swaps)
    return (keys_one, values_one, keys_two, values_two)


def solution(mesh):
    split = Mesh(mesh.devices.reshape(SIZES), AXES)
    whole, line = ("x", "z", "h"), ("l", "c")
    sharded = P(whole, line)
    in_specs = (sharded,) * 2 + (P(),) * 4 + (sharded,) * 4 + (P(whole),) * 3
    return jax.shard_map(
        on_device, mesh=split, in_specs=in_specs, out_specs=(sharded,) * 4, check_vma=False
    )
```

```python
import jax
import jax.numpy as jnp
from jax import lax
from jax.experimental import pallas as pl
from jax.experimental.pallas import tpu as pltpu
from jax.sharding import Mesh
from jax.sharding import PartitionSpec as P

HD = 128
EPS = 1e-06
AXES = ("x", "z", "h", "l", "c")
SIZES = (4, 8, 2, 4, 2)


def move(value, axes, place):
    sizes = [SIZES[AXES.index(axis)] for axis in axes]
    total = 1
    for size in sizes:
        total *= size

    def coordinates(index):
        found = []
        for size in reversed(sizes):
            found.append(index % size)
            index //= size
        return found[::-1]

    def flat(at):
        index = 0
        for size, one in zip(sizes, at):
            index = index * size + one
        return index

    pairs = [(index, flat(place(*coordinates(index)))) for index in range(total)]
    return lax.ppermute(value, axes, pairs)


def head_norm(raw_key, key_gain):
    mean = jnp.mean(raw_key * raw_key, axis=-1, keepdims=True)
    return raw_key * lax.rsqrt(mean + EPS) * key_gain


def row_scale(squares, width, live):
    return jnp.where(live, lax.rsqrt(squares / width + EPS), 0.0)


def square_sums(x):
    wide = x.astype(jnp.float32)
    wide = wide * wide
    return sum(wide[:, first : first + HD] for first in range(0, x.shape[1], HD))


def project(place, layer, x_refs, w_ref, gain_ref, squares=0.0):
    l, c, length = place[0], place[1], place[2]
    raw = 0.0
    known = len(x_refs) // 2 if isinstance(squares, jax.Array) else 0
    for i in range(0, len(x_refs), 2):
        x = jnp.concatenate([x_ref[...] for x_ref in x_refs[i : i + 2]], axis=1)
        cores = pl.ds((c ^ (i // 4)) * 4, 4)
        w = [w_ref[cores, l ^ (i % 4), layer], w_ref[cores, l ^ (i % 4 + 1), layer]]
        w = jnp.concatenate([half.reshape(-1, 2 * HD) for half in w])
        raw += jnp.dot(x, w, preferred_element_type=jnp.float32)
        if i >= known:
            squares += square_sums(x)
    squares = jnp.sum(squares, axis=-1, keepdims=True)
    live = lax.broadcasted_iota(jnp.int32, squares.shape, 0) < length
    raw *= row_scale(squares, len(x_refs) * x_refs[0].shape[1], live)
    return head_norm(raw[:, :HD], gain_ref[...]).astype(jnp.bfloat16), raw[:, HD:].astype(jnp.bfloat16)


def squares_kernel(*refs):
    refs[-1][...] = sum(square_sums(x_ref[...]) for x_ref in refs[:-1])


def one_kernel(place, *refs):
    key_ref, value_ref = refs[10:]
    key_ref[...], value_ref[...] = project(place, 0, refs[:8], refs[8], refs[9])


def two_kernel(place, *refs):
    out_ref = refs[11]
    keys, values = project(place, 1, refs[:8], refs[8], refs[9], refs[10][...])
    out_ref[:, :HD], out_ref[:, HD:] = keys, values


def finish_two_kernel(place, own_ref, *refs):
    swap_refs, (key_ref, value_ref) = refs[:3], refs[3:]
    rows = own_ref.shape[0]
    pair_bit, is_old = place[3], place[4] == 1
    own = own_ref[...]
    received = jnp.where(pair_bit == 1, swap_refs[1][...], swap_refs[0][...])
    received = jnp.where(pair_bit == 2, swap_refs[2][...], received)
    for first, part in ((0, own), (rows, received)):
        part = jnp.where(is_old, part, jnp.zeros_like(part))
        key_ref[first : first + rows, :] = part[:, :HD]
        value_ref[first : first + rows, :] = part[:, HD:]


VMEM = pl.BlockSpec(memory_space=pltpu.VMEM)
SMEM = pl.BlockSpec(memory_space=pltpu.SMEM)
PARAMS = pltpu.CompilerParams(vmem_limit_bytes=24 * 1024 * 1024)


def on_device(
    x_one,
    x_two,
    norm_one,
    norm_two,
    key_gain_one,
    key_gain_two,
    wk_one,
    wv_one,
    wk_two,
    wv_two,
    lengths,
    new_flag,
    partner,
):
    rows, width = x_one.shape
    depth = wk_one.shape[0]
    x, z, h, l, c = [lax.axis_index(axis) for axis in AXES]
    slot = (x * 8 + z) * 2 + h
    pair_bit = jnp.bitwise_xor(partner[0], slot)
    is_old = (new_flag[0] == 0).astype(jnp.int32)
    def scaled(gain, w_key, w_value):
        mine = lax.dynamic_slice(gain, (slot * depth,), (depth,))[:, None]
        both = jnp.concatenate([w_key, w_value], axis=1).astype(jnp.float32)
        return (both * mine).astype(jnp.bfloat16)

    here = jnp.stack([scaled(norm_one, wk_one, wv_one), scaled(norm_two, wk_two, wv_two)])
    there = move(here, ("h",), lambda h: (h ^ 1,))
    weights = jnp.concatenate(
        [jnp.where(h == 0, here, there), jnp.where(h == 0, there, here)], axis=1
    )
    weights = lax.all_gather(lax.all_gather(weights, "x"), "z")

    def from_line(block, apart):
        return move(block, ("l",), lambda l: (l ^ apart,))

    def from_core(block):
        return move(block, ("c",), lambda c: (c ^ 1,))

    two_far = from_line(x_two, 2)
    two_near = from_line(x_two, 1)
    two_blocks = [x_two, two_near, two_far, from_line(two_far, 1)]
    squares_two = pl.pallas_call(
        squares_kernel,
        out_shape=jax.ShapeDtypeStruct((rows, HD), jnp.float32),
        in_specs=[VMEM] * 4,
        out_specs=VMEM,
        compiler_params=PARAMS,
        cost_estimate=pl.CostEstimate(flops=90_000_000_000, bytes_accessed=0, transcendentals=0),
        name="squares_two",
    )(*two_blocks)
    two_blocks += [from_core(block) for block in two_blocks]
    one_far = from_line(x_one, 2)
    x_first, two_near = lax.optimization_barrier((x_one, two_near))
    one_near = from_line(x_first, 1)
    one_last = from_line(one_far, 1)
    place = jnp.stack([l, c, lengths[0], pair_bit, is_old]).astype(jnp.int32)

    flops = 2 * rows * 8 * width * 2 * HD
    moved = 8 * rows * width * 2 + 8 * width * 2 * HD * 2
    cost = pl.CostEstimate(flops=flops, bytes_accessed=moved, transcendentals=0)
    both_two = pl.pallas_call(
        two_kernel,
        out_shape=jax.ShapeDtypeStruct((rows, 2 * HD), jnp.bfloat16),
        in_specs=[SMEM] + [VMEM] * 11,
        out_specs=VMEM,
        compiler_params=PARAMS,
        cost_estimate=cost,
        name="layer_two",
    )(place, *two_blocks, weights, key_gain_two.reshape(1, HD), squares_two)
    swaps = [
        move(both_two, ("z",), lambda z: (z ^ 2,)),
        move(both_two, ("h",), lambda h: (h ^ 1,)),
        move(both_two, ("z",), lambda z: (z ^ 1,)),
    ]

    one_last, both_two = lax.optimization_barrier((one_last, both_two))
    one_blocks = [x_one, one_near, one_far, one_last]
    one_blocks += [from_core(block) for block in one_blocks]
    keys_one, values_one = pl.pallas_call(
        one_kernel,
        out_shape=(jax.ShapeDtypeStruct((rows, HD), jnp.bfloat16),) * 2,
        in_specs=[SMEM] + [VMEM] * 10,
        out_specs=(VMEM, VMEM),
        compiler_params=PARAMS,
        cost_estimate=cost,
        name="layer_one",
    )(place, *one_blocks, weights, key_gain_one.reshape(1, HD))
    place, keys_one, values_one = lax.optimization_barrier((place, keys_one, values_one))
    keys_two, values_two = pl.pallas_call(
        finish_two_kernel,
        out_shape=(jax.ShapeDtypeStruct((2 * rows, HD), jnp.bfloat16),) * 2,
        in_specs=[SMEM] + [VMEM] * 4,
        out_specs=(VMEM, VMEM),
        compiler_params=PARAMS,
        name="finish_two",
    )(place, both_two, *swaps)
    return (keys_one, values_one, keys_two, values_two)


def solution(mesh):
    split = Mesh(mesh.devices.reshape(SIZES), AXES)
    whole, line = ("x", "z", "h"), ("l", "c")
    sharded = P(whole, line)
    in_specs = (sharded,) * 2 + (P(),) * 4 + (sharded,) * 4 + (P(whole),) * 3
    return jax.shard_map(
        on_device, mesh=split, in_specs=in_specs, out_specs=(sharded,) * 4, check_vma=False
    )
```

```python
import jax
import jax.numpy as jnp
from jax import lax
from jax.experimental import pallas as pl
from jax.experimental.pallas import tpu as pltpu
from jax.sharding import Mesh
from jax.sharding import PartitionSpec as P

HD = 128
EPS = 1e-06
AXES = ("x", "z", "h", "l", "c")
SIZES = (4, 8, 2, 4, 2)


def move(value, axes, place):
    sizes = [SIZES[AXES.index(axis)] for axis in axes]
    total = 1
    for size in sizes:
        total *= size

    def coordinates(index):
        found = []
        for size in reversed(sizes):
            found.append(index % size)
            index //= size
        return found[::-1]

    def flat(at):
        index = 0
        for size, one in zip(sizes, at):
            index = index * size + one
        return index

    pairs = [(index, flat(place(*coordinates(index)))) for index in range(total)]
    return lax.ppermute(value, axes, pairs)


def head_norm(raw_key, key_gain):
    mean = jnp.mean(raw_key * raw_key, axis=-1, keepdims=True)
    return raw_key * lax.rsqrt(mean + EPS) * key_gain


def row_scale(squares, width, live):
    return jnp.where(live, lax.rsqrt(squares / width + EPS), 0.0)


def square_sums(x):
    wide = x.astype(jnp.float32)
    wide = wide * wide
    return sum(wide[:, first : first + HD] for first in range(0, x.shape[1], HD))


def project(place, layer, x_refs, w_ref, gain_ref, squares=0.0):
    l, c, length = place[0], place[1], place[2]
    raw = 0.0
    known = len(x_refs) // 2 if isinstance(squares, jax.Array) else 0
    for i in range(0, len(x_refs), 2):
        x = jnp.concatenate([x_ref[...] for x_ref in x_refs[i : i + 2]], axis=1)
        cores = pl.ds((c ^ (i // 4)) * 4, 4)
        w = [w_ref[cores, l ^ (i % 4), layer], w_ref[cores, l ^ (i % 4 + 1), layer]]
        w = jnp.concatenate([half.reshape(-1, 2 * HD) for half in w])
        raw += jnp.dot(x, w, preferred_element_type=jnp.float32)
        if i >= known:
            squares += square_sums(x)
    squares = jnp.sum(squares, axis=-1, keepdims=True)
    live = lax.broadcasted_iota(jnp.int32, squares.shape, 0) < length
    raw *= row_scale(squares, len(x_refs) * x_refs[0].shape[1], live)
    return head_norm(raw[:, :HD], gain_ref[...]).astype(jnp.bfloat16), raw[:, HD:].astype(jnp.bfloat16)


def squares_kernel(*refs):
    refs[-1][...] = sum(square_sums(x_ref[...]) for x_ref in refs[:-1])


def one_kernel(place, *refs):
    key_ref, value_ref = refs[10:]
    key_ref[...], value_ref[...] = project(place, 0, refs[:8], refs[8], refs[9])


def two_kernel(place, *refs):
    out_ref = refs[11]
    keys, values = project(place, 1, refs[:8], refs[8], refs[9], refs[10][...])
    out_ref[:, :HD], out_ref[:, HD:] = keys, values


def finish_two_kernel(place, own_ref, *refs):
    swap_refs, (key_ref, value_ref) = refs[:3], refs[3:]
    rows = own_ref.shape[0]
    pair_bit, is_old = place[3], place[4] == 1
    own = own_ref[...]
    received = jnp.where(pair_bit == 1, swap_refs[1][...], swap_refs[0][...])
    received = jnp.where(pair_bit == 2, swap_refs[2][...], received)
    for first, part in ((0, own), (rows, received)):
        part = jnp.where(is_old, part, jnp.zeros_like(part))
        key_ref[first : first + rows, :] = part[:, :HD]
        value_ref[first : first + rows, :] = part[:, HD:]


VMEM = pl.BlockSpec(memory_space=pltpu.VMEM)
SMEM = pl.BlockSpec(memory_space=pltpu.SMEM)
PARAMS = pltpu.CompilerParams(vmem_limit_bytes=24 * 1024 * 1024)


def on_device(
    x_one,
    x_two,
    norm_one,
    norm_two,
    key_gain_one,
    key_gain_two,
    wk_one,
    wv_one,
    wk_two,
    wv_two,
    lengths,
    new_flag,
    partner,
):
    rows, width = x_one.shape
    depth = wk_one.shape[0]
    x, z, h, l, c = [lax.axis_index(axis) for axis in AXES]
    slot = (x * 8 + z) * 2 + h
    pair_bit = jnp.bitwise_xor(partner[0], slot)
    is_old = (new_flag[0] == 0).astype(jnp.int32)
    def scaled(gain, w_key, w_value):
        mine = lax.dynamic_slice(gain, (slot * depth,), (depth,))[:, None]
        both = jnp.concatenate([w_key, w_value], axis=1).astype(jnp.float32)
        return (both * mine).astype(jnp.bfloat16)

    here = jnp.stack([scaled(norm_one, wk_one, wv_one), scaled(norm_two, wk_two, wv_two)])
    there = move(here, ("h",), lambda h: (h ^ 1,))
    weights = jnp.concatenate(
        [jnp.where(h == 0, here, there), jnp.where(h == 0, there, here)], axis=1
    )
    weights = lax.all_gather(lax.all_gather(weights, "x"), "z")

    def from_line(block, apart):
        return move(block, ("l",), lambda l: (l ^ apart,))

    def from_core(block):
        return move(block, ("c",), lambda c: (c ^ 1,))

    two_far = from_line(x_two, 2)
    two_near = from_line(x_two, 1)
    two_blocks = [x_two, two_near, two_far, from_line(two_far, 1)]
    squares_two = pl.pallas_call(
        squares_kernel,
        out_shape=jax.ShapeDtypeStruct((rows, HD), jnp.float32),
        in_specs=[VMEM] * 4,
        out_specs=VMEM,
        compiler_params=PARAMS,
        cost_estimate=pl.CostEstimate(flops=90_000_000_000, bytes_accessed=0, transcendentals=0),
        name="squares_two",
    )(*two_blocks)
    two_blocks += [from_core(block) for block in two_blocks]
    one_far = from_line(x_one, 2)
    one_near = from_line(x_one, 1)
    one_last = from_line(one_far, 1)
    place = jnp.stack([l, c, lengths[0], pair_bit, is_old]).astype(jnp.int32)

    flops = 2 * rows * 8 * width * 2 * HD
    moved = 8 * rows * width * 2 + 8 * width * 2 * HD * 2
    cost = pl.CostEstimate(flops=flops, bytes_accessed=moved, transcendentals=0)
    both_two = pl.pallas_call(
        two_kernel,
        out_shape=jax.ShapeDtypeStruct((rows, 2 * HD), jnp.bfloat16),
        in_specs=[SMEM] + [VMEM] * 11,
        out_specs=VMEM,
        compiler_params=PARAMS,
        cost_estimate=cost,
        name="layer_two",
    )(place, *two_blocks, weights, key_gain_two.reshape(1, HD), squares_two)
    swaps = [
        move(both_two, ("z",), lambda z: (z ^ 2,)),
        move(both_two, ("h",), lambda h: (h ^ 1,)),
        move(both_two, ("z",), lambda z: (z ^ 1,)),
    ]

    one_last, both_two = lax.optimization_barrier((one_last, both_two))
    one_blocks = [x_one, one_near, one_far, one_last]
    one_blocks += [from_core(block) for block in one_blocks]
    keys_one, values_one = pl.pallas_call(
        one_kernel,
        out_shape=(jax.ShapeDtypeStruct((rows, HD), jnp.bfloat16),) * 2,
        in_specs=[SMEM] + [VMEM] * 10,
        out_specs=(VMEM, VMEM),
        compiler_params=PARAMS,
        cost_estimate=cost,
        name="layer_one",
    )(place, *one_blocks, weights, key_gain_one.reshape(1, HD))
    place, keys_one, values_one = lax.optimization_barrier((place, keys_one, values_one))
    keys_two, values_two = pl.pallas_call(
        finish_two_kernel,
        out_shape=(jax.ShapeDtypeStruct((2 * rows, HD), jnp.bfloat16),) * 2,
        in_specs=[SMEM] + [VMEM] * 4,
        out_specs=(VMEM, VMEM),
        compiler_params=PARAMS,
        name="finish_two",
    )(place, both_two, *swaps)
    return (keys_one, values_one, keys_two, values_two)


def solution(mesh):
    split = Mesh(mesh.devices.reshape(SIZES), AXES)
    whole, line = ("x", "z", "h"), ("l", "c")
    sharded = P(whole, line)
    in_specs = (sharded,) * 2 + (P(),) * 4 + (sharded,) * 4 + (P(whole),) * 3
    return jax.shard_map(
        on_device, mesh=split, in_specs=in_specs, out_specs=(sharded,) * 4, check_vma=False
    )
```
